32 devices in a mesh: dp: 16 (over z, y, x), mp: 2 (over core).
Axes of the slice: x: 2, y: 2, z: 4, core: 2. Of those that a mesh axis runs over, the one named last changes fastest.
Arguments:
- tokens: bfloat16 [16, 1024, 1024], P('dp', 'mp'), may hold values from -6 to 6
- memory: bfloat16 [16, 512, 1024], P('dp', 'mp'), may hold values from -6 to 6
- segments: int32 [16, 1024], P('dp'), may hold values from 0 to 8, as said below
- sources: int32 [16, 512], P('dp'), may hold values from 0 to 8, as said below
- gains: float32 [3, 1024], replicated, may hold values from 0.5 to 1.5
- biases: float32 [6, 1024], replicated, may hold values from -1.8 to 1.8
- head_biases: float32 [4, 1024], P(None, 'mp'), may hold values from -1.8 to 1.8
- self_proj: float32 [3, 1024, 1024], P(None, 'dp', 'mp'), may hold values from -0.1875 to 0.1875
- self_out: float32 [1024, 1024], P('mp', 'dp'), may hold values from -0.75 to 0.75
- cross_query: float32 [1024, 1024], P('dp', 'mp'), may hold values from -0.1875 to 0.1875
- cross_kv: float32 [2, 1024, 1024], P(None, 'dp', 'mp'), may hold values from -0.1875 to 0.1875
- cross_out: float32 [1024, 1024], P('mp', 'dp'), may hold values from -0.75 to 0.75
- up_weight: float32 [1024, 8192], P('dp', 'mp'), may hold values from -0.1875 to 0.1875
- up_bias: float32 [8192], P('mp'), may hold values from -1.8 to 1.8
- down_weight: float32 [8192, 1024], P('mp', 'dp'), may hold values from -0.0625 to 0.0625
- cotangent: bfloat16 [16, 1024, 1024], P('dp', 'mp'), may hold values from -6 to 6
Outputs:
- layer_out: bfloat16 [16, 1024, 1024], P('dp', 'mp')
- d_tokens: bfloat16 [16, 1024, 1024], P('dp', 'mp')
- d_memory: bfloat16 [16, 512, 1024], P('dp', 'mp')
- d_gains: float32 [3, 1024], replicated
- d_biases: float32 [6, 1024], replicated
- d_head_biases: float32 [4, 1024], P(None, 'mp')
- d_self_proj: float32 [3, 1024, 1024], P(None, 'dp', 'mp')
- d_self_out: float32 [1024, 1024], P('mp', 'dp')
- d_cross_query: float32 [1024, 1024], P('dp', 'mp')
- d_cross_kv: float32 [2, 1024, 1024], P(None, 'dp', 'mp')
- d_cross_out: float32 [1024, 1024], P('mp', 'dp')
- d_up_weight: float32 [1024, 8192], P('dp', 'mp')
- d_up_bias: float32 [8192], P('mp')
- d_down_weight: float32 [8192, 1024], P('mp', 'dp')
The draws below stay inside these ranges and needn't reach their ends.
Inputs may be any that keep to these rules, and one draw needn't show every extreme that they name: `segments`: in each sequence the document numbers never fall; documents 1 to 8 are followed by 1 to 128 positions of padding 0 at the end; one document covers the positions from 384 to 639. `sources`: in each memory the source numbers 1 to 8 follow in order, each on one position or more, then 1 to 64 positions of padding 0 at the end.
All inputs are finite; a program needn't handle non-finite values.
Results may differ from the reference program's by a relative error of at most 0.02.
Values may be sent and summed in bfloat16 or wider, within the bound.
No kernel may reach another device: no remote copies, remote signals or barrier semaphores. Data moves between devices by JAX's collectives and lax.ppermute only.
A program may use at most 192 MiB of HBM per device.

```python
import math
import jax
import jax.numpy as jnp
from jax import lax

D = 1024
HEADS = 16
HEAD = 64
FF = 8192
LEN = 1024
MEM = 512
DOCS = 8
SEQS = 16


def draw_segments(key, part):
    key = jax.random.fold_in(key, 11)
    key_pad, key_first, key_second = jax.random.split(key, 3)
    eighth = LEN // 8
    padding = jax.random.randint(key_pad, (SEQS, 1), 1, eighth + 1)
    first = jax.random.randint(key_first, (SEQS, DOCS // 2 - 1), 0, 1024)
    second = jax.random.randint(key_second, (SEQS, DOCS // 2), 0, 1024)
    cuts_low = 1 + first * first // 1024 * (3 * eighth - 1) // 1024
    cuts_high = 5 * eighth + second * second // 1024 * (2 * eighth - 1) // 1024
    cuts = jnp.concatenate([cuts_low, cuts_high], axis=1)
    positions = jnp.arange(LEN, dtype=jnp.int32)
    number = 1 + jnp.sum((positions[None, :, None] >= cuts[:, None, :]).astype(jnp.int32), axis=-1)
    return jnp.where(positions[None, :] < LEN - padding, number, 0).astype(jnp.int32)


def draw_sources(key, part):
    key = jax.random.fold_in(key, 23)
    key_pad, key_cut = jax.random.split(key, 2)
    padding = jax.random.randint(key_pad, (SEQS, 1), 1, MEM // 8 + 1)
    raw = jax.random.randint(key_cut, (SEQS, DOCS - 1), 0, MEM - MEM // 8 - DOCS + 1)
    cuts = jnp.sort(raw, axis=-1) + 1 + jnp.arange(DOCS - 1, dtype=jnp.int32)[None, :]
    positions = jnp.arange(MEM, dtype=jnp.int32)
    number = 1 + jnp.sum((positions[None, :, None] >= cuts[:, None, :]).astype(jnp.int32), axis=-1)
    return jnp.where(positions[None, :] < MEM - padding, number, 0).astype(jnp.int32)


def block_scale(rng, shape, cuts, smallest, largest):
    gain = 1.0
    for position, shards_of in cuts:
        steps = jax.random.uniform(jax.random.fold_in(jax.random.fold_in(rng, 6), position), (shards_of,), jnp.float32, smallest / len(cuts), largest / len(cuts))
        gain = gain * jnp.repeat(jnp.exp(steps), shape[position] // shards_of).reshape((-1,) + (1,) * (len(shape) - 1 - position))
    return gain


def noise(stream_key, shape, scale, most, pieces=(), kind=jnp.bfloat16):
    values = scale * jax.random.normal(stream_key, shape, jnp.float32)
    if pieces:
        values = values * block_scale(stream_key, shape, pieces, -0.22, 0.18)
    return jnp.clip(values, -most, most).astype(kind)


def setup_inputs(seed: int = 0) -> dict:
    splits = jax.random.split(jax.random.key(seed), 17)
    tokens = noise(splits[0], (SEQS, LEN, D), 1.0, 6.0, ((0, 16), (1, 2)))
    memory = noise(splits[1], (SEQS, MEM, D), 1.0, 6.0, ((0, 16), (1, 2)))
    segments = draw_segments(jax.random.fold_in(splits[16], 71), 0)
    sources = draw_sources(jax.random.fold_in(splits[16], 71), 0)
    gains = jnp.clip(1.0 + 0.1 * jax.random.normal(splits[4], (3, D), jnp.float32), 0.5, 1.5)
    biases = noise(splits[5], (6, D), 0.3, 1.8, (), jnp.float32)
    head_biases = noise(splits[6], (4, D), 0.3, 1.8, ((1, 2),), jnp.float32)
    self_proj = noise(splits[7], (3, D, D), D ** -0.5, 0.1875, ((1, 16), (2, 2)), jnp.float32)
    self_out = noise(splits[8], (D, D), (D // 16) ** -0.5, 0.75, ((0, 2), (1, 16)), jnp.float32)
    cross_query = noise(splits[9], (D, D), D ** -0.5, 0.1875, ((0, 16), (1, 2)), jnp.float32)
    cross_kv = noise(splits[10], (2, D, D), D ** -0.5, 0.1875, ((1, 16), (2, 2)), jnp.float32)
    cross_out = noise(splits[11], (D, D), (D // 16) ** -0.5, 0.75, ((0, 2), (1, 16)), jnp.float32)
    up_weight = noise(splits[12], (D, FF), D ** -0.5, 0.1875, ((0, 16), (1, 2)), jnp.float32)
    up_bias = noise(splits[13], (FF,), 0.3, 1.8, ((0, 2),), jnp.float32)
    down_weight = noise(splits[14], (FF, D), FF ** -0.5, 0.0625, ((0, 2), (1, 16)), jnp.float32)
    cotangent = noise(splits[15], (SEQS, LEN, D), 1.0, 6.0, ((0, 16), (1, 2)))
    return dict(tokens=tokens, memory=memory, segments=segments, sources=sources, gains=gains, biases=biases, head_biases=head_biases, self_proj=self_proj, self_out=self_out, cross_query=cross_query, cross_kv=cross_kv, cross_out=cross_out, up_weight=up_weight, up_bias=up_bias, down_weight=down_weight, cotangent=cotangent)


@jax.custom_vjp
def low(v):
    return lax.optimization_barrier(v.astype(jnp.bfloat16)).astype(jnp.float32)

@jax.custom_vjp
def low_back(v):
    return v

def low_keep(v):
    return (low(v), None)

def low_pass(kept, grad):
    return (grad,)

def back_keep(v):
    return (v, None)

def back_low(kept, grad):
    return (low(grad),)
low.defvjp(low_keep, low_pass)
low_back.defvjp(back_keep, back_low)

def round_both(values):
    return low(low_back(values))

def normalize(values, gain_row, shift_row):
    average = lax.optimization_barrier(jnp.mean(values, axis=-1, keepdims=True))
    centred = values - average
    spread = lax.optimization_barrier(jnp.mean(centred * centred, axis=-1, keepdims=True))
    return centred * lax.rsqrt(spread + 1e-05) * gain_row + shift_row

def product(operand, weight):
    return jnp.einsum('srk,kn->srn', operand, weight, precision=lax.Precision.HIGHEST)

def attention(queries, key_rows, value_rows, allowed):
    members, length = (queries.shape[0], queries.shape[1])
    width = key_rows.shape[1]
    query_heads = queries.reshape(members, length, HEADS, HEAD)
    key_heads = key_rows.reshape(members, width, HEADS, HEAD)
    value_heads = value_rows.reshape(members, width, HEADS, HEAD)
    scores = low_back(jnp.einsum('sqhe,skhe->shqk', query_heads, key_heads, precision=lax.Precision.HIGHEST) * (1.0 / math.sqrt(HEAD)))
    scores = jnp.where(allowed[:, None], scores, -1e+30)
    chance = low(jax.nn.softmax(scores, axis=-1))
    result = jnp.einsum('shqk,skhe->sqhe', chance, value_heads, precision=lax.Precision.HIGHEST)
    return round_both(result.reshape(members, length, HEADS * HEAD))

def decoder_layer(tokens_in, memory_in, params, segments, sources):
    gains, biases, head_biases, self_proj, self_out, cross_query, cross_kv, cross_out, up_weight, up_bias, down_weight = params
    positions = jnp.arange(tokens_in.shape[1])
    self_allowed = (segments[:, :, None] == segments[:, None, :]) & (positions[None, :, None] >= positions[None, None, :])
    cross_allowed = segments[:, :, None] == sources[:, None, :]
    norm_one = low(normalize(tokens_in, gains[0], biases[0]))
    queries = round_both(product(norm_one, low(self_proj[0])) + head_biases[0])
    key_rows = round_both(product(norm_one, low(self_proj[1])))
    value_rows = round_both(product(norm_one, low(self_proj[2])) + head_biases[1])
    attended = attention(queries, key_rows, value_rows, self_allowed)
    after_self = tokens_in + low_back(product(attended, low(self_out))) + biases[1]
    norm_two = low(normalize(after_self, gains[1], biases[2]))
    cross_queries = round_both(product(norm_two, low(cross_query)) + head_biases[2])
    cross_keys = round_both(product(memory_in, low(cross_kv[0])))
    cross_values = round_both(product(memory_in, low(cross_kv[1])) + head_biases[3])
    cross_attended = attention(cross_queries, cross_keys, cross_values, cross_allowed)
    after_cross = after_self + low_back(product(cross_attended, low(cross_out))) + biases[3]
    norm_three = low(normalize(after_cross, gains[2], biases[4]))
    hidden_pre = low_back(product(norm_three, low(up_weight)) + up_bias)
    hidden_act = low(jax.nn.gelu(hidden_pre, approximate=False))
    return after_cross + low_back(product(hidden_act, low(down_weight))) + biases[5]

def reference(tokens, memory, segments, sources, gains, biases, head_biases, self_proj, self_out, cross_query, cross_kv, cross_out, up_weight, up_bias, down_weight, cotangent):
    params = (gains, biases, head_biases, self_proj, self_out, cross_query, cross_kv, cross_out, up_weight, up_bias, down_weight)
    group = 2 if SEQS % 2 == 0 else 1
    steps_count = SEQS // group

    def regroup(values):
        return values.reshape((steps_count, group) + values.shape[1:])
    inputs = (regroup(tokens), regroup(memory), regroup(segments), regroup(sources), regroup(cotangent))
    zeros = jax.tree.map(lambda item: jnp.zeros(item.shape, jnp.float32), params)

    def one_step(summed, item):
        tok_rows, mem_rows, seg_rows, src_rows, cot_rows = item

        def forward(tokens_in, memory_in, weights_in):
            return decoder_layer(tokens_in, memory_in, weights_in, seg_rows, src_rows)
        result, backward = jax.vjp(forward, tok_rows.astype(jnp.float32), mem_rows.astype(jnp.float32), params)
        grad_tok, grad_mem, grad_params = backward(cot_rows.astype(jnp.float32))
        summed = jax.tree.map(lambda first, second: first + second, summed, grad_params)
        return (summed, (result.astype(jnp.bfloat16), grad_tok.astype(jnp.bfloat16), grad_mem.astype(jnp.bfloat16)))
    summed, (results, grad_tokens, grad_memory) = lax.scan(one_step, zeros, inputs)
    d_gains, d_biases, d_head_biases, d_self_proj, d_self_out, d_cross_query, d_cross_kv, d_cross_out, d_up_weight, d_up_bias, d_down_weight = summed
    layer_out = results.reshape(SEQS, LEN, D)
    d_tokens = grad_tokens.reshape(SEQS, LEN, D)
    d_memory = grad_memory.reshape(SEQS, MEM, D)
    return (layer_out, d_tokens, d_memory, d_gains, d_biases, d_head_biases, d_self_proj, d_self_out, d_cross_query, d_cross_kv, d_cross_out, d_up_weight, d_up_bias, d_down_weight)
```

```python
import functools
import math

import jax
import jax.numpy as jnp
from jax import lax
from jax.experimental import pallas as pl
from jax.experimental.pallas import tpu as pltpu
from jax.sharding import Mesh
from jax.sharding import PartitionSpec as P

HEAD = 64
PAIR = 2 * HEAD
F32 = jnp.float32
BF16 = jnp.bfloat16
VMEM_LIMIT = 56 * 1024 * 1024
MASKED = -1e30


def dot(left, right, left_dim, right_dim):
    return lax.dot_general(
        left, right, (((left_dim,), (right_dim,)), ((), ())), preferred_element_type=F32
    )


def normalize(values, gain_row, shift_row):
    average = jnp.mean(values, axis=-1, keepdims=True)
    centred = values - average
    spread = jnp.mean(centred * centred, axis=-1, keepdims=True)
    return centred * lax.rsqrt(spread + 1e-05) * gain_row + shift_row


def row_total(rows):
    return jnp.sum(rows.astype(F32), axis=0)


def swap(values, axis):
    return lax.ppermute(values, axis, [(0, 1), (1, 0)])


def in_order(own, other, index, dim):
    first = jnp.where(index == 0, own, other)
    second = jnp.where(index == 0, other, own)
    return first, second


def both(own, axis, dim):
    return jnp.concatenate(in_order(own, swap(own, axis), lax.axis_index(axis), dim), dim)


def gather_line(block, axis, size):
    if size > 4:
        return lax.all_gather(block, axis, axis=0, tiled=False)
    me = lax.axis_index(axis)
    whole = jnp.zeros((size,) + block.shape, block.dtype)
    whole = lax.dynamic_update_index_in_dim(whole, block, me, 0)
    for step in range(1, size):
        got = lax.ppermute(block, axis, [(at, (at + step) % size) for at in range(size)])
        whole = lax.dynamic_update_index_in_dim(whole, got, lax.rem(me - step + size, size), 0)
    return whole


def scatter_line(blocks, axis, size):
    if size > 4:
        return lax.psum_scatter(blocks.astype(F32), axis, scatter_dimension=0, tiled=False)
    me = lax.axis_index(axis)
    total = lax.dynamic_index_in_dim(blocks, me, 0, False).astype(F32)
    for step in range(1, size):
        block = lax.dynamic_index_in_dim(blocks, lax.rem(me + step, size), 0, False)
        got = lax.ppermute(block, axis, [(at, (at + step) % size) for at in range(size)])
        total = total + got.astype(F32)
    return total


def gather_pair(blocks, axis, dim):
    own, other = blocks, swap(blocks, axis)
    return jnp.stack(in_order(own, other, lax.axis_index(axis), dim), dim)


def scatter_pair(blocks, axis, dim):
    me = lax.axis_index(axis)
    keep = lax.dynamic_index_in_dim(blocks, me, dim, False)
    send = lax.dynamic_index_in_dim(blocks, 1 - me, dim, False)
    return (keep.astype(F32) + swap(send, axis).astype(F32)).astype(BF16)


def halves(values, low):
    zero = jnp.zeros_like(values)
    return jnp.where(low, values, zero), jnp.where(low, zero, values)


def low_lanes():
    return lax.broadcasted_iota(jnp.int32, (1, PAIR), 1) < HEAD


def forward_kernel(causal, tile, q_ref, k_ref, v_ref, row_ref, col_ref, o_ref, log_ref):
    length, width = q_ref.shape[0], k_ref.shape[0]
    low = low_lanes()
    for number in range(length // tile):
        rows = pl.ds(number * tile, tile)
        q_parts = halves(q_ref[rows, :] * 0.125, low)
        spans = [(0, width)]
        if causal:
            spans = [(0, number * tile)] if number else []
            spans.append((number * tile, tile))
        allowed = []
        for start, size in spans:
            same = row_ref[rows, :] == col_ref[:, pl.ds(start, size)]
            if causal and start == number * tile:
                same = same & (
                    lax.broadcasted_iota(jnp.int32, (tile, size), 0)
                    >= lax.broadcasted_iota(jnp.int32, (tile, size), 1)
                )
            allowed.append(same)
        result = jnp.zeros((tile, PAIR), F32)
        tops, sums = [], []
        for half in range(2):
            scores = []
            for (start, size), same in zip(spans, allowed):
                part = dot(q_parts[half], k_ref[pl.ds(start, size), :], 1, 1)
                scores.append(jnp.where(same, part, MASKED))
            top = functools.reduce(
                jnp.maximum, [jnp.max(part, axis=1, keepdims=True) for part in scores]
            )
            summed = jnp.zeros((tile, 1), F32)
            for (start, size), part in zip(spans, scores):
                chance = jnp.exp(part - top)
                summed = summed + jnp.sum(chance, axis=1, keepdims=True)
                v_part = halves(v_ref[pl.ds(start, size), :], low)[half]
                result = result + dot(chance.astype(BF16), v_part, 1, 0)
            tops.append(top)
            sums.append(summed)
        total = jnp.where(low, sums[0], sums[1])
        o_ref[rows, :] = (result / total).astype(BF16)
        logs = jnp.where(low, tops[0], tops[1]) + jnp.log(total)
        flipped = logs.T
        log_ref[0, 0:1, rows] = flipped[0:1, :]
        log_ref[0, 1:2, rows] = flipped[HEAD : HEAD + 1, :]


def backward_kernel(
    causal,
    tile,
    q_ref,
    k_ref,
    v_ref,
    o_ref,
    g_ref,
    log_ref,
    row_ref,
    col_ref,
    dq_ref,
    dk_ref,
    dv_ref,
    dk_sum,
    dv_sum,
):
    length, width = q_ref.shape[0], k_ref.shape[0]
    low = low_lanes()
    dk_sum[...] = jnp.zeros_like(dk_sum)
    dv_sum[...] = jnp.zeros_like(dv_sum)
    for number in range(length // tile):
        rows = pl.ds(number * tile, tile)
        q_parts = halves(q_ref[rows, :] * 0.125, low)
        grad = g_ref[rows, :]
        g_parts = halves(grad, low)
        product = (grad.astype(F32) * o_ref[rows, :].astype(F32)).T
        deltas = [
            jnp.sum(product[:HEAD], axis=0, keepdims=True),
            jnp.sum(product[HEAD:], axis=0, keepdims=True),
        ]
        dq = jnp.zeros((tile, PAIR), F32)
        for other in range(number + 1 if causal else width // tile):
            cols = pl.ds(other * tile, tile)
            same = col_ref[cols, :] == row_ref[:, rows]
            if causal and other == number:
                same = same & (
                    lax.broadcasted_iota(jnp.int32, (tile, tile), 1)
                    >= lax.broadcasted_iota(jnp.int32, (tile, tile), 0)
                )
            key, value = k_ref[cols, :], v_ref[cols, :]
            k_parts = halves(key, low)
            dk = jnp.zeros((tile, PAIR), F32)
            dv = jnp.zeros((tile, PAIR), F32)
            for half in range(2):
                scores = jnp.where(same, dot(key, q_parts[half], 1, 1), MASKED)
                chance = jnp.exp(scores - log_ref[0, half : half + 1, rows])
                dv = dv + dot(chance.astype(BF16), g_parts[half], 1, 0)
                change = dot(value, g_parts[half], 1, 1)
                inner = (chance * (change - deltas[half])).astype(BF16)
                dk = dk + dot(inner, q_parts[half], 1, 0)
                dq = dq + dot(inner, k_parts[half], 0, 0)
            dk_sum[cols, :] += dk
            dv_sum[cols, :] += dv
        dq_ref[rows, :] = (dq * 0.125).astype(BF16)
    dk_ref[...] = dk_sum[...].astype(BF16)
    dv_ref[...] = dv_sum[...].astype(BF16)


def attention_cost(length, width, features, products):
    return pl.CostEstimate(
        flops=8 * products * length * width * features,
        bytes_accessed=2 * features * (2 * length + 2 * width),
        transcendentals=length * width * features // HEAD,
    )


def attend(queries, keys, values, row_docs, col_docs, causal):
    length, features = queries.shape
    width = keys.shape[0]
    tile = min(256, length)
    at = lambda size: pl.BlockSpec((size, PAIR), lambda pair: (0, pair))
    fixed = lambda shape: pl.BlockSpec(shape, lambda pair: (0, 0))
    return pl.pallas_call(
        functools.partial(forward_kernel, causal, tile),
        grid=(features // PAIR,),
        in_specs=[at(length), at(width), at(width), fixed((length, 1)), fixed((1, width))],
        out_specs=[at(length), pl.BlockSpec((1, 2, length), lambda pair: (pair, 0, 0))],
        out_shape=[
            jax.ShapeDtypeStruct((length, features), BF16),
            jax.ShapeDtypeStruct((features // PAIR, 2, length), F32),
        ],
        compiler_params=pltpu.CompilerParams(vmem_limit_bytes=VMEM_LIMIT),
        cost_estimate=attention_cost(length, width, features, 2),
    )(queries, keys, values, row_docs[:, None], col_docs[None, :])


def attend_back(queries, keys, values, result, grad, logs, row_docs, col_docs, causal):
    length, features = queries.shape
    width = keys.shape[0]
    tile = min(256, length, width)
    at = lambda size: pl.BlockSpec((size, PAIR), lambda pair: (0, pair))
    fixed = lambda shape: pl.BlockSpec(shape, lambda pair: (0, 0))
    return pl.pallas_call(
        functools.partial(backward_kernel, causal, tile),
        grid=(features // PAIR,),
        in_specs=[
            at(length),
            at(width),
            at(width),
            at(length),
            at(length),
            pl.BlockSpec((1, 2, length), lambda pair: (pair, 0, 0)),
            fixed((1, length)),
            fixed((width, 1)),
        ],
        out_specs=[at(length), at(width), at(width)],
        out_shape=[
            jax.ShapeDtypeStruct((length, features), BF16),
            jax.ShapeDtypeStruct((width, features), BF16),
            jax.ShapeDtypeStruct((width, features), BF16),
        ],
        scratch_shapes=[pltpu.VMEM((width, PAIR), F32), pltpu.VMEM((width, PAIR), F32)],
        compiler_params=pltpu.CompilerParams(vmem_limit_bytes=VMEM_LIMIT),
        cost_estimate=attention_cost(length, width, features, 5),
    )(queries, keys, values, result, grad, logs, row_docs[None, :], col_docs[:, None])


def gelu_and_slope(values):
    tail = jnp.exp(values * values * -0.5)
    step = 1.0 / (1.0 + (0.3275911 * math.sqrt(0.5)) * jnp.abs(values))
    series = 1.061405429
    for factor in (-1.453152027, 1.421413741, -0.284496736, 0.254829592):
        series = series * step + factor
    outside = (0.5 * series) * step * tail
    below = jnp.where(values >= 0, 1.0 - outside, outside)
    return values * below, below + values * tail * (1.0 / math.sqrt(2.0 * math.pi))


def hidden_kernel(piece, x_ref, g_ref, up_ref, down_ref, bias_ref, act_ref, grad_ref):
    for number in range(x_ref.shape[0] // piece):
        rows = pl.ds(number * piece, piece)
        before = dot(x_ref[rows, :], up_ref[...], 1, 0) + bias_ref[...]
        act, slope = gelu_and_slope(before)
        act_ref[rows, :] = act.astype(BF16)
        raw = dot(g_ref[rows, :], down_ref[...], 1, 0)
        grad_ref[rows, :] = (raw * slope).astype(BF16)


def hidden_parts(normed, grad, up, down_rows, bias_row):
    rows, features = normed.shape
    hidden = up.shape[1]
    tile = min(512, hidden)
    whole = pl.BlockSpec((rows, features), lambda step: (0, 0))
    piece = lambda height: pl.BlockSpec((height, tile), lambda step: (0, step))
    return pl.pallas_call(
        functools.partial(hidden_kernel, min(256, rows)),
        grid=(hidden // tile,),
        in_specs=[whole, whole, piece(features), piece(features), piece(1)],
        out_specs=[piece(rows), piece(rows)],
        out_shape=[jax.ShapeDtypeStruct((rows, hidden), BF16)] * 2,
        compiler_params=pltpu.CompilerParams(vmem_limit_bytes=VMEM_LIMIT),
        cost_estimate=pl.CostEstimate(
            flops=4 * rows * features * hidden,
            bytes_accessed=4 * (rows * features + features * hidden + rows * hidden),
            transcendentals=rows * hidden,
        ),
    )(normed, grad, up, down_rows, bias_row)


def per_device(
    line,
    tokens,
    memory,
    segments,
    sources,
    gains,
    biases,
    head_biases,
    self_proj,
    self_out,
    cross_query,
    cross_kv,
    cross_out,
    up_weight,
    up_bias,
    down_weight,
    cotangent,
):
    at_x, at_core = lax.axis_index("x"), lax.axis_index("core")
    row_docs, col_docs = segments[0], sources[0]
    half_rows, features = tokens.shape[1:]
    heads_width = self_out.shape[0]
    part_rows = self_out.shape[1]
    hidden_part = up_weight.shape[1] // 2

    def gather_attention(shard):
        blocks = gather_line(shard, "z", line)
        blocks = gather_pair(blocks, "y", 1)
        blocks = gather_pair(blocks, "x", 2)
        return blocks.reshape(features, shard.shape[1])

    def gather_hidden(shard):
        keep = lax.dynamic_slice_in_dim(shard, at_x * hidden_part, hidden_part, 1)
        send = lax.dynamic_slice_in_dim(shard, (1 - at_x) * hidden_part, hidden_part, 1)
        rows = jnp.concatenate(in_order(keep, swap(send, "x"), at_x, 0), 0)
        blocks = gather_pair(gather_line(rows, "z", line), "y", 1)
        return blocks.reshape(features, hidden_part)

    def scatter_attention(grad):
        blocks = grad.reshape(line, 2, 2, part_rows, grad.shape[1])
        blocks = scatter_pair(blocks, "x", 2)
        blocks = scatter_pair(blocks, "y", 1)
        return scatter_line(blocks, "z", line)

    def scatter_hidden(grad):
        blocks = scatter_pair(grad.reshape(line, 2, 2 * part_rows, hidden_part), "y", 1)
        rows = scatter_line(blocks, "z", line).reshape(2, part_rows, hidden_part)
        keep = lax.dynamic_index_in_dim(rows, at_x, 0, False)
        send = lax.dynamic_index_in_dim(rows, 1 - at_x, 0, False).astype(BF16)
        return jnp.concatenate(in_order(keep, swap(send, "x").astype(F32), at_x, 1), 1)

    def own_rows(values):
        return lax.dynamic_slice_in_dim(values, at_core * half_rows, half_rows, 0)

    def summed(partial):
        short = partial.astype(BF16)
        return short.astype(F32) + swap(short, "core").astype(F32)

    def summed_rows(partial):
        short = partial.astype(BF16)
        pieces = short.reshape(2, short.shape[0] // 2, short.shape[1])
        keep = lax.dynamic_index_in_dim(pieces, at_core, 0, False)
        send = lax.dynamic_index_in_dim(pieces, 1 - at_core, 0, False)
        return keep.astype(F32) + swap(send, "core").astype(F32)

    def short(part):
        return part.astype(BF16)

    first = gather_attention(
        jnp.concatenate([short(self_proj[0]), short(self_proj[1]), short(self_proj[2])], 1)
    )
    second = gather_attention(
        jnp.concatenate(
            [
                short(self_out).T,
                short(cross_query),
                short(cross_kv[0]),
                short(cross_kv[1]),
                short(cross_out).T,
            ],
            1,
        )
    )
    up = gather_hidden(short(up_weight))
    down_rows = gather_hidden(short(down_weight).T)
    column = lambda whole, number: whole[:, number * heads_width : (number + 1) * heads_width]
    w_query, w_key, w_value = (column(first, number) for number in range(3))
    w_out, w_cross_query, w_cross_key, w_cross_value, w_cross_out = (
        column(second, number) for number in range(5)
    )
    bias_part = lax.dynamic_slice_in_dim(up_bias, at_x * hidden_part, hidden_part, 0)[None, :]

    rows_in = both(tokens[0], "core", 0).astype(F32)
    mem_rows = both(memory[0], "core", 0)
    grad_mine = cotangent[0]
    grad_theirs = swap(grad_mine, "x")
    grad_own = both(grad_mine, "core", 0)
    grad_other = both(grad_theirs, "core", 0)

    norm_one, back_one = jax.vjp(normalize, rows_in, gains[0], biases[0])
    norm_one = short(norm_one)
    queries = short(dot(norm_one, w_query, 1, 0) + head_biases[0])
    keys = short(dot(norm_one, w_key, 1, 0))
    values = short(dot(norm_one, w_value, 1, 0) + head_biases[1])
    attended, logs_self = attend(queries, keys, values, row_docs, row_docs, True)
    after_self = rows_in + summed(dot(attended, w_out, 1, 1)) + biases[1]
    norm_two, back_two = jax.vjp(normalize, after_self, gains[1], biases[2])
    norm_two = short(norm_two)
    cross_queries = short(dot(norm_two, w_cross_query, 1, 0) + head_biases[2])
    cross_keys = short(dot(mem_rows, w_cross_key, 1, 0))
    cross_values = short(dot(mem_rows, w_cross_value, 1, 0) + head_biases[3])
    cross_attended, logs_cross = attend(
        cross_queries, cross_keys, cross_values, row_docs, col_docs, False
    )
    after_cross = after_self + summed(dot(cross_attended, w_cross_out, 1, 1)) + biases[3]
    after_cross_mine = own_rows(after_cross)
    norm_three, back_three = jax.vjp(normalize, after_cross_mine, gains[2], biases[4])
    norm_three = short(norm_three)

    norm_own = both(norm_three, "core", 0)
    norm_other = both(swap(norm_three, "x"), "core", 0)
    act_own, hid_own = hidden_parts(norm_own, grad_own, up, down_rows, bias_part)
    act_other, hid_other = hidden_parts(norm_other, grad_other, up, down_rows, bias_part)

    def over_pair(own, other):
        own_part, other_part = summed_rows(own), summed_rows(other)
        return own_part + swap(short(other_part), "x").astype(F32)

    d_norm_three = over_pair(dot(hid_own, up, 1, 1), dot(hid_other, up, 1, 1))
    d_down = short(dot(grad_own, act_own, 0, 0) + dot(grad_other, act_other, 0, 0))
    d_up = short(dot(norm_own, hid_own, 0, 0) + dot(norm_other, hid_other, 0, 0))
    d_down_weight = scatter_hidden(d_down).T
    d_up_weight = scatter_hidden(d_up)
    fed = over_pair(dot(act_own, down_rows, 1, 1), dot(act_other, down_rows, 1, 1))
    layer_out = short(after_cross_mine + fed + biases[5])
    d_up_bias = row_total(hid_own) + row_total(hid_other)

    grad_rows = grad_mine.astype(F32)
    d_bias_five = row_total(grad_rows)
    back_rows, d_gain_two, d_bias_four = back_three(d_norm_three)
    d_cross_res = grad_rows + back_rows
    d_bias_three = row_total(d_cross_res)
    res_rows = both(short(d_cross_res), "core", 0)
    d_cross_out = dot(res_rows, cross_attended, 0, 0)
    d_cross_att = short(dot(res_rows, w_cross_out, 1, 0))
    cq_grad, ck_grad, cv_grad = attend_back(
        cross_queries,
        cross_keys,
        cross_values,
        cross_attended,
        d_cross_att,
        logs_cross,
        row_docs,
        col_docs,
        False,
    )
    d_norm_two = summed(dot(cq_grad, w_cross_query, 1, 1))
    d_memory = short(
        summed_rows(dot(ck_grad, w_cross_key, 1, 1) + dot(cv_grad, w_cross_value, 1, 1))
    )
    d_cross_weights = scatter_attention(
        jnp.concatenate(
            [
                short(d_cross_out),
                short(dot(norm_two, cq_grad, 0, 0)),
                short(dot(mem_rows, ck_grad, 0, 0)),
                short(dot(mem_rows, cv_grad, 0, 0)),
            ],
            1,
        )
    )
    back_rows, d_gain_one, d_bias_two = back_two(d_norm_two)
    d_self_res = res_rows.astype(F32) + back_rows
    d_bias_one = row_total(d_self_res)
    self_rows = short(d_self_res)
    d_self_out = short(dot(self_rows, attended, 0, 0))
    d_attended = short(dot(self_rows, w_out, 1, 0))
    q_grad, k_grad, v_grad = attend_back(
        queries, keys, values, attended, d_attended, logs_self, row_docs, row_docs, True
    )
    d_self_weights = scatter_attention(
        jnp.concatenate(
            [
                d_self_out,
                short(dot(norm_one, q_grad, 0, 0)),
                short(dot(norm_one, k_grad, 0, 0)),
                short(dot(norm_one, v_grad, 0, 0)),
            ],
            1,
        )
    )
    d_norm_one = summed(
        dot(q_grad, w_query, 1, 1) + dot(k_grad, w_key, 1, 1) + dot(v_grad, w_value, 1, 1)
    )
    back_rows, d_gain_zero, d_bias_zero = back_one(d_norm_one)
    d_tokens = short(own_rows(d_self_res + back_rows))

    small = jnp.stack(
        [
            d_gain_zero * 0.5,
            d_gain_one * 0.5,
            d_gain_two,
            d_bias_zero * 0.5,
            d_bias_one * 0.5,
            d_bias_two * 0.5,
            d_bias_three,
            d_bias_four,
            d_bias_five,
        ]
    )
    head_rows = jnp.stack(
        [row_total(q_grad), row_total(v_grad), row_total(cq_grad), row_total(cv_grad)]
    )
    head_place = jnp.zeros((4, 2, heads_width), F32)
    head_place = lax.dynamic_update_slice(head_place, head_rows[:, None], (0, at_core, 0))
    bias_place = jnp.zeros((2, 2, hidden_part), F32)
    bias_place = lax.dynamic_update_slice(
        bias_place, d_up_bias[None, None], (at_core, at_x, 0)
    )
    totals = lax.psum(
        jnp.concatenate([small.reshape(-1), head_place.reshape(-1), bias_place.reshape(-1)]),
        ("z", "y", "x", "core"),
    )
    count, head_count = small.size, head_place.size
    small = totals[:count].reshape(small.shape)
    head_place = totals[count : count + head_count].reshape(head_place.shape)
    bias_place = totals[count + head_count :].reshape(2, 2 * hidden_part)
    d_head_biases = lax.dynamic_index_in_dim(head_place, at_core, 1, False)
    d_up_bias = lax.dynamic_index_in_dim(bias_place, at_core, 0, False)

    return (
        layer_out[None],
        d_tokens[None],
        d_memory[None],
        small[:3],
        small[3:],
        d_head_biases,
        jnp.stack([column(d_self_weights, number) for number in (1, 2, 3)]),
        column(d_self_weights, 0).T,
        column(d_cross_weights, 1),
        jnp.stack([column(d_cross_weights, number) for number in (2, 3)]),
        column(d_cross_weights, 0).T,
        d_up_weight,
        d_up_bias,
        d_down_weight,
    )


def solution(mesh):
    members, cores = mesh.devices.shape
    line = members // 4
    parts = Mesh(mesh.devices.reshape(line, 2, 2, cores), ("z", "y", "x", "core"))
    dp = ("z", "y", "x")
    in_specs = (
        P(dp, "core", None),
        P(dp, "core", None),
        P(dp, None),
        P(dp, None),
        P(),
        P(),
        P(None, "core"),
        P(None, dp, "core"),
        P("core", dp),
        P(dp, "core"),
        P(None, dp, "core"),
        P("core", dp),
        P(dp, "core"),
        P("core"),
        P("core", dp),
        P(dp, "core", None),
    )
    out_specs = (
        P(dp, "core", None),
        P(dp, "core", None),
        P(dp, "core", None),
        P(),
        P(),
        P(None, "core"),
        P(None, dp, "core"),
        P("core", dp),
        P(dp, "core"),
        P(None, dp, "core"),
        P("core", dp),
        P(dp, "core"),
        P("core"),
        P("core", dp),
    )
    return jax.shard_map(
        functools.partial(per_device, line),
        mesh=parts,
        in_specs=in_specs,
        out_specs=out_specs,
        check_vma=False,
    )
```

```python
import functools
import math

import jax
import jax.numpy as jnp
from jax import lax
from jax.experimental import pallas as pl
from jax.experimental.pallas import tpu as pltpu
from jax.sharding import Mesh
from jax.sharding import PartitionSpec as P

HEAD = 64
PAIR = 2 * HEAD
F32 = jnp.float32
BF16 = jnp.bfloat16
VMEM_LIMIT = 56 * 1024 * 1024
MASKED = -1e30


def dot(left, right, left_dim, right_dim):
    return lax.dot_general(
        left, right, (((left_dim,), (right_dim,)), ((), ())), preferred_element_type=F32
    )


def normalize(values, gain_row, shift_row):
    average = jnp.mean(values, axis=-1, keepdims=True)
    centred = values - average
    spread = jnp.mean(centred * centred, axis=-1, keepdims=True)
    return centred * lax.rsqrt(spread + 1e-05) * gain_row + shift_row


def row_total(rows):
    return jnp.sum(rows.astype(F32), axis=0)


def after(values, *earlier):
    return lax.optimization_barrier((values, earlier))[0]


def swap(values, axis):
    return lax.ppermute(values, axis, [(0, 1), (1, 0)])


def join_pair(own, other, index, dim):
    size = own.shape[dim]
    whole = jnp.zeros(own.shape[:dim] + (2 * size,) + own.shape[dim + 1 :], own.dtype)
    whole = lax.dynamic_update_slice_in_dim(whole, own, index * size, dim)
    return lax.dynamic_update_slice_in_dim(whole, other, (1 - index) * size, dim)


def stack_pair(own, other, index, dim):
    return join_pair(jnp.expand_dims(own, dim), jnp.expand_dims(other, dim), index, dim)


AXES = ("zh", "zl", "y", "x")


class Gather:
    def __init__(self, shard, order, *earlier):
        shard = after(shard, *earlier) if earlier else shard
        self.blocks = shard.reshape((1, 1, 1, 1) + shard.shape)
        self.order = list(order)
        self.send()

    def send(self):
        self.axis = self.order.pop(0)
        if lax.axis_size(self.axis) == 2:
            self.got = swap(self.blocks, self.axis)
        else:
            dim = AXES.index(self.axis)
            self.got = lax.all_gather(self.blocks, self.axis, axis=dim, tiled=True)

    def parts(self, *earlier):
        got = after(self.got, *earlier) if earlier else self.got
        dim = AXES.index(self.axis)
        if lax.axis_size(self.axis) != 2:
            return [(got, dim, 0)]
        me = lax.axis_index(self.axis)
        return [(self.blocks, dim, me), (got, dim, 1 - me)]

    def join(self, *earlier):
        self.blocks = assemble([self], *earlier)
        return self.blocks

    def step(self, *earlier, first=()):
        blocks = self.join(*earlier)
        if first:
            self.blocks = after(blocks, *first)
        self.send()
        return blocks


def assemble(gathers, *earlier):
    pieces = [gather.parts(*earlier) for gather in gathers]
    if len(gathers) == 1 and len(pieces[0]) == 1:
        return pieces[0][0][0]
    shape = list(pieces[0][0][0].shape)
    for part in pieces[0][1:]:
        shape[part[1]] += part[0].shape[part[1]]
    shape[-1] = sum(piece[0][0].shape[-1] for piece in pieces)
    whole = jnp.zeros(shape, BF16)
    column = 0
    for piece in pieces:
        for block, dim, index in piece:
            start = [0] * len(shape)
            start[dim] = index * block.shape[dim]
            start[-1] = column
            whole = lax.dynamic_update_slice(whole, block, start)
        column += piece[0][0].shape[-1]
    return whole


class Scatter:
    def __init__(self, blocks, order):
        self.order = list(order)
        self.left = [axis for axis in AXES if axis in order]
        self.send(blocks)

    def send(self, blocks):
        axis = self.order.pop(0)
        dim = self.left.index(axis)
        self.left.pop(dim)
        if lax.axis_size(axis) == 2:
            self.keep, self.got = halve_send(blocks, axis, dim)
        else:
            self.keep = lax.psum_scatter(
                blocks.astype(F32), axis, scatter_dimension=dim, tiled=False
            )
            self.got = jnp.zeros((1,), F32)

    def step(self, *earlier):
        got = after(self.got, *earlier) if earlier else self.got
        total = self.keep.astype(F32) + got.astype(F32)
        if self.order:
            total = total.astype(BF16)
            self.send(total)
        return total


def line_total(values):
    if lax.axis_size("zh") != 2:
        return lax.psum(values, "zh")
    return values + swap(values, "zh")


def halve_send(blocks, axis, dim):
    me = lax.axis_index(axis)
    keep = lax.dynamic_index_in_dim(blocks, me, dim, False)
    send = lax.dynamic_index_in_dim(blocks, 1 - me, dim, False)
    return keep, swap(send, axis)


def halves(values, low):
    zero = jnp.zeros_like(values)
    return jnp.where(low, values, zero), jnp.where(low, zero, values)


def low_lanes():
    return lax.broadcasted_iota(jnp.int32, (1, PAIR), 1) < HEAD


def forward_kernel(causal, tile, q_ref, k_ref, v_ref, row_ref, col_ref, o_ref, log_ref):
    length, width = q_ref.shape[0], k_ref.shape[0]
    low = low_lanes()
    for number in range(length // tile):
        rows = pl.ds(number * tile, tile)
        q_parts = halves(q_ref[rows, :] * 0.125, low)
        spans = [(0, width)]
        if causal:
            spans = [(0, number * tile)] if number else []
            spans.append((number * tile, tile))
        allowed = []
        for start, size in spans:
            same = row_ref[rows, :] == col_ref[:, pl.ds(start, size)]
            if causal and start == number * tile:
                same = same & (
                    lax.broadcasted_iota(jnp.int32, (tile, size), 0)
                    >= lax.broadcasted_iota(jnp.int32, (tile, size), 1)
                )
            allowed.append(same)
        result = jnp.zeros((tile, PAIR), F32)
        tops, sums = [], []
        for half in range(2):
            scores = []
            for (start, size), same in zip(spans, allowed):
                part = dot(q_parts[half], k_ref[pl.ds(start, size), :], 1, 1)
                scores.append(jnp.where(same, part, MASKED))
            top = functools.reduce(
                jnp.maximum, [jnp.max(part, axis=1, keepdims=True) for part in scores]
            )
            summed = jnp.zeros((tile, 1), F32)
            for (start, size), part in zip(spans, scores):
                chance = jnp.exp(part - top)
                summed = summed + jnp.sum(chance, axis=1, keepdims=True)
                v_part = halves(v_ref[pl.ds(start, size), :], low)[half]
                result = result + dot(chance.astype(BF16), v_part, 1, 0)
            tops.append(top)
            sums.append(summed)
        total = jnp.where(low, sums[0], sums[1])
        o_ref[rows, :] = (result / total).astype(BF16)
        logs = jnp.where(low, tops[0], tops[1]) + jnp.log(total)
        flipped = logs.T
        log_ref[0, 0:1, rows] = flipped[0:1, :]
        log_ref[0, 1:2, rows] = flipped[HEAD : HEAD + 1, :]


def backward_kernel(
    causal,
    tile,
    columns,
    q_ref,
    k_ref,
    v_ref,
    o_ref,
    g_ref,
    log_ref,
    row_ref,
    col_ref,
    *outs,
):
    dq_ref, dkv_ref, dk_sum, dv_sum = outs[0], outs[-3], outs[-2], outs[-1]
    length, width = q_ref.shape[0], k_ref.shape[0]
    low = low_lanes()
    q_at, k_at, v_at = (
        pl.ds(pl.multiple_of(column + pl.program_id(0) * PAIR, PAIR), PAIR) for column in columns
    )
    dk_sum[...] = jnp.zeros_like(dk_sum)
    dv_sum[...] = jnp.zeros_like(dv_sum)
    for number in range(length // tile):
        rows = pl.ds(number * tile, tile)
        q_parts = halves(q_ref[rows, :] * 0.125, low)
        grad = g_ref[rows, :]
        g_parts = halves(grad, low)
        product = (grad.astype(F32) * o_ref[rows, :].astype(F32)).T
        deltas = [
            jnp.sum(product[:HEAD], axis=0, keepdims=True),
            jnp.sum(product[HEAD:], axis=0, keepdims=True),
        ]
        dq = jnp.zeros((tile, PAIR), F32)
        for other in range(number + 1 if causal else width // tile):
            cols = pl.ds(other * tile, tile)
            same = col_ref[cols, :] == row_ref[:, rows]
            if causal and other == number:
                same = same & (
                    lax.broadcasted_iota(jnp.int32, (tile, tile), 1)
                    >= lax.broadcasted_iota(jnp.int32, (tile, tile), 0)
                )
            key, value = k_ref[cols, :], v_ref[cols, :]
            k_parts = halves(key, low)
            dk = jnp.zeros((tile, PAIR), F32)
            dv = jnp.zeros((tile, PAIR), F32)
            for half in range(2):
                scores = jnp.where(same, dot(key, q_parts[half], 1, 1), MASKED)
                chance = jnp.exp(scores - log_ref[0, half : half + 1, rows])
                dv = dv + dot(chance.astype(BF16), g_parts[half], 1, 0)
                change = dot(value, g_parts[half], 1, 1)
                inner = (chance * (change - deltas[half])).astype(BF16)
                dk = dk + dot(inner, q_parts[half], 1, 0)
                dq = dq + dot(inner, k_parts[half], 0, 0)
            dk_sum[cols, :] += dk
            dv_sum[cols, :] += dv
        dq_ref[rows, q_at] = (dq * 0.125).astype(BF16)
    dkv_ref[:, k_at] = dk_sum[...].astype(BF16)
    dkv_ref[:, v_at] = dv_sum[...].astype(BF16)


SMALL_COST = pl.CostEstimate(flops=1024, bytes_accessed=1024, transcendentals=0)


def pair_at(size, first):
    return pl.BlockSpec((size, PAIR), lambda pair: (0, first + pair))


def fixed(shape):
    return pl.BlockSpec(shape, lambda pair: (0, 0))


def logs_at(length):
    return pl.BlockSpec((1, 2, length), lambda pair: (pair, 0, 0))


def attend(query_set, key_set, columns, features, row_docs, col_docs, causal):
    length, width = query_set.shape[0], key_set.shape[0]
    tile = min(256, length)
    return pl.pallas_call(
        functools.partial(forward_kernel, causal, tile),
        grid=(features // PAIR,),
        in_specs=[
            pair_at(length, columns[0] // PAIR),
            pair_at(width, columns[1] // PAIR),
            pair_at(width, columns[2] // PAIR),
            fixed((length, 1)),
            fixed((1, width)),
        ],
        out_specs=[pair_at(length, 0), logs_at(length)],
        out_shape=[
            jax.ShapeDtypeStruct((length, features), BF16),
            jax.ShapeDtypeStruct((features // PAIR, 2, length), F32),
        ],
        compiler_params=pltpu.CompilerParams(vmem_limit_bytes=VMEM_LIMIT),
        cost_estimate=SMALL_COST,
    )(query_set, key_set, key_set, row_docs[:, None], col_docs[None, :])


def attend_back(
    query_set, key_set, columns, features, result, grad, logs, row_docs, col_docs, causal
):
    length, width = query_set.shape[0], key_set.shape[0]
    tile = min(256, length, width)
    outs = [jax.ShapeDtypeStruct(query_set.shape, BF16)]
    if key_set is not query_set:
        outs.append(jax.ShapeDtypeStruct(key_set.shape, BF16))
    return pl.pallas_call(
        functools.partial(backward_kernel, causal, tile, columns),
        grid=(features // PAIR,),
        in_specs=[
            pair_at(length, columns[0] // PAIR),
            pair_at(width, columns[1] // PAIR),
            pair_at(width, columns[2] // PAIR),
            pair_at(length, 0),
            pair_at(length, 0),
            logs_at(length),
            fixed((1, length)),
            fixed((width, 1)),
        ],
        out_specs=[fixed(out.shape) for out in outs],
        out_shape=outs,
        scratch_shapes=[pltpu.VMEM((width, PAIR), F32), pltpu.VMEM((width, PAIR), F32)],
        compiler_params=pltpu.CompilerParams(vmem_limit_bytes=VMEM_LIMIT),
        cost_estimate=SMALL_COST,
    )(query_set, key_set, key_set, result, grad, logs, row_docs[None, :], col_docs[:, None])


def gelu_and_slope(values):
    tail = jnp.exp(values * values * -0.5)
    step = 1.0 / (1.0 + (0.3275911 * math.sqrt(0.5)) * jnp.abs(values))
    series = 1.061405429
    for factor in (-1.453152027, 1.421413741, -0.284496736, 0.254829592):
        series = series * step + factor
    outside = (0.5 * series) * step * tail
    below = jnp.where(values >= 0, 1.0 - outside, outside)
    return values * below, below + values * tail * (1.0 / math.sqrt(2.0 * math.pi))


def hidden_kernel(piece, x_ref, g_ref, up_ref, down_ref, bias_ref, act_ref, grad_ref):
    for number in range(x_ref.shape[0] // piece):
        rows = pl.ds(number * piece, piece)
        before = dot(x_ref[rows, :], up_ref[...], 1, 0) + bias_ref[...]
        act, slope = gelu_and_slope(before)
        act_ref[rows, :] = act.astype(BF16)
        raw = dot(g_ref[rows, :], down_ref[...], 1, 0)
        grad_ref[rows, :] = (raw * slope).astype(BF16)


def hidden_parts(normed, grad, up, down_rows, bias_row):
    rows, features = normed.shape
    hidden = up.shape[1]
    tile = min(512, hidden)
    whole = pl.BlockSpec((rows, features), lambda step: (0, 0))
    piece = lambda height: pl.BlockSpec((height, tile), lambda step: (0, step))
    return pl.pallas_call(
        functools.partial(hidden_kernel, min(256, rows)),
        grid=(hidden // tile,),
        in_specs=[whole, whole, piece(features), piece(features), piece(1)],
        out_specs=[piece(rows), piece(rows)],
        out_shape=[jax.ShapeDtypeStruct((rows, hidden), BF16)] * 2,
        compiler_params=pltpu.CompilerParams(vmem_limit_bytes=VMEM_LIMIT),
        cost_estimate=SMALL_COST,
    )(normed, grad, up, down_rows, bias_row)


def per_device(
    tokens,
    memory,
    segments,
    sources,
    gains,
    biases,
    head_biases,
    self_proj,
    self_out,
    cross_query,
    cross_kv,
    cross_out,
    up_weight,
    up_bias,
    down_weight,
    cotangent,
):
    at_x, at_y, at_core = (lax.axis_index(axis) for axis in ("x", "y", "core"))
    row_docs, col_docs = segments[0], sources[0]
    half_rows, features = tokens.shape[1:]
    width = self_out.shape[0]
    part_rows = self_out.shape[1]
    hidden_part = up_weight.shape[1] // 2
    chunk = hidden_part // 2

    def short(part):
        return part.astype(BF16)

    def own_rows(values):
        return lax.dynamic_slice_in_dim(values, at_core * half_rows, half_rows, 0)

    def core_join(own, other):
        return join_pair(own, other, at_core, 0)

    def summed(partial):
        brief = short(partial)
        return brief.astype(F32) + swap(brief, "core").astype(F32)

    def summed_rows(partial):
        brief = short(partial)
        keep, got = halve_send(brief.reshape((2, -1) + brief.shape[1:]), "core", 0)
        return keep.astype(F32) + got.astype(F32)

    first = jnp.concatenate([short(self_proj[number]) for number in range(3)], 1)
    second = jnp.concatenate([short(self_out).T, short(cross_query)], 1)
    third = jnp.concatenate([short(cross_kv[0]), short(cross_kv[1]), short(cross_out).T], 1)
    cut = first.shape[1] // 2
    line_first, x_first = ("zh", "zl", "y", "x"), ("x", "y", "zh", "zl")
    g_one = Gather(first[:, :cut], line_first)
    g_two = Gather(first[:, cut:], x_first)
    tokens_core = swap(tokens[0], "core")
    grad_mine = cotangent[0]

    def pair_rows(shard):
        keep = lax.dynamic_slice_in_dim(shard, at_x * hidden_part, hidden_part, 1)
        send = lax.dynamic_slice_in_dim(shard, (1 - at_x) * hidden_part, hidden_part, 1)
        return join_pair(keep, swap(send, "x"), at_x, 0)

    rows_in = core_join(tokens[0], tokens_core).astype(F32)
    norm_one, back_one = jax.vjp(normalize, rows_in, gains[0], biases[0])
    norm_one = short(norm_one)

    one = g_one.step()
    two = g_two.step()
    up_rows, down_part = (pair_rows(short(up_weight)), pair_rows(short(down_weight).T))
    hidden_rows = [up_rows[:, :chunk], up_rows[:, chunk:], down_part[:, :chunk], down_part[:, chunk:]]
    hidden_order = ("zh", "zl", "y")
    g_out = Gather(second, line_first, one)
    one = g_one.step()
    two = g_two.step()
    out = g_out.step(first=(one,))
    g_kv = Gather(third, line_first, out)
    memory_core = swap(after(memory[0], two), "core")
    one = g_one.step()
    out = g_out.step(first=(one,))
    kv = g_kv.step(first=(out,))
    two = g_two.step()
    kv = g_kv.step(two)
    w_first = assemble([g_one, g_two]).reshape(features, -1)
    g_up = Gather(hidden_rows[0], hidden_order, w_first)
    out = g_out.step(first=(w_first,))

    bias_first = jnp.concatenate([head_biases[0], jnp.zeros((width,), F32), head_biases[1]])
    qkv = short(dot(after(norm_one, out, kv), w_first, 1, 0) + bias_first)
    up_one = g_up.step(qkv)
    g_up_two = Gather(hidden_rows[1], hidden_order, up_one)
    kv = g_kv.step(qkv)

    self_columns, cross_columns = (0, width, 2 * width), (0, 0, width)
    attended, logs_self = attend(
        after(qkv, up_one, kv), qkv, self_columns, width, row_docs, row_docs, True
    )

    w_second = g_out.join(attended).reshape(features, -1)
    grad_core = swap(after(grad_mine, attended), "core")
    up_one = g_up.step(attended)
    up_two = g_up_two.step(attended)
    g_down = Gather(hidden_rows[2], hidden_order, up_two)
    w_out, w_cross_query = w_second[:, :width], w_second[:, width:]

    after_self = rows_in + summed(dot(after(attended, up_one, up_two), w_out, 1, 1)) + biases[1]
    norm_two, back_two = jax.vjp(normalize, after_self, gains[1], biases[2])
    norm_two = short(norm_two)
    up_two = g_up_two.step(norm_two)
    down_one = g_down.step(norm_two)
    g_down_two = Gather(hidden_rows[3], hidden_order, down_one)
    cross_queries = short(
        dot(after(norm_two, up_two, down_one), w_cross_query, 1, 0) + head_biases[2]
    )

    w_third = g_kv.join(cross_queries).reshape(features, -1)
    grad_theirs = swap(after(grad_mine, w_third), "x")
    w_cross_kv, w_cross_out = w_third[:, : 2 * width], w_third[:, 2 * width :]
    mem_rows = core_join(memory[0], memory_core)
    bias_kv = jnp.concatenate([jnp.zeros((width,), F32), head_biases[3]])
    cross_kvs = short(dot(mem_rows, w_cross_kv, 1, 0) + bias_kv)
    down_one = g_down.step(cross_kvs)
    down_two = g_down_two.step(cross_kvs)
    cross_attended, logs_cross = attend(
        after(cross_queries, down_one, down_two, g_up.got),
        cross_kvs,
        cross_columns,
        width,
        row_docs,
        col_docs,
        False,
    )
    down_two = g_down_two.step(cross_attended)
    after_cross = (
        after_self
        + summed(dot(after(cross_attended, down_two, g_up_two.got), w_cross_out, 1, 1))
        + biases[3]
    )
    after_cross_mine = own_rows(after_cross)
    norm_three, back_three = jax.vjp(normalize, after_cross_mine, gains[2], biases[4])
    norm_three = short(norm_three)
    norm_theirs = swap(norm_three, "x")
    norm_own = core_join(norm_three, swap(after(norm_three, grad_theirs), "core"))
    grad_own = core_join(grad_mine, grad_core)
    grad_other = core_join(grad_theirs, swap(grad_theirs, "core"))

    up = assemble([g_up, g_up_two]).reshape(features, hidden_part)
    down_rows = assemble([g_down, g_down_two], norm_three).reshape(features, hidden_part)
    bias_part = lax.dynamic_slice_in_dim(up_bias, at_x * hidden_part, hidden_part, 0)[None, :]

    act_own, hid_own = hidden_parts(norm_own, grad_own, up, down_rows, bias_part)
    norm_theirs = after(norm_theirs, act_own)
    norm_other = core_join(norm_theirs, swap(norm_theirs, "core"))
    act_other, hid_other = hidden_parts(norm_other, grad_other, up, down_rows, bias_part)

    back_own = dot(hid_own, up, 1, 1)
    back_other = dot(hid_other, up, 1, 1)
    part_other = summed_rows(back_other)
    theirs_three = swap(short(part_other), "x")
    part_own = summed_rows(back_own)

    hidden_way, all_way = ("y", "zl", "zh"), ("x", "y", "zl", "zh")

    def scatter(grad, way):
        return Scatter(grad.reshape(up_blocks[: len(way)] + (-1, grad.shape[1])), way)

    up_blocks = tuple(lax.axis_size(axis) for axis in AXES)

    chunks = []
    ready = [part_own]
    for left_own, left_other, right_own, right_other in (
        (grad_own, grad_other, act_own, act_other),
        (norm_own, norm_other, hid_own, hid_other),
    ):
        for half in range(2):
            columns = slice(half * chunk, (half + 1) * chunk)
            grad = short(
                dot(after(left_own, *ready), right_own[:, columns], 0, 0)
                + dot(after(left_other, *ready), right_other[:, columns], 0, 0)
            )
            if len(chunks) > 1:
                grad = after(grad, chunks[len(chunks) - 2].got)
            chunks.append(scatter(grad, hidden_way))
            ready = [grad]
    one, two, three, four = chunks

    moved = one.step(*ready)
    fed_other = summed_rows(dot(after(act_other, moved), down_rows, 1, 1))
    fed_own = dot(after(act_own, moved, fed_other), down_rows, 1, 1)
    d_norm_three = part_own + after(theirs_three, fed_own).astype(F32)
    grad_rows = grad_mine.astype(F32)
    d_bias_five = row_total(grad_rows)
    back_rows, d_gain_two, d_bias_four = back_three(d_norm_three)
    d_cross_res = grad_rows + back_rows
    d_bias_three = row_total(d_cross_res)
    res_mine = short(d_cross_res)
    moved = [one.step(res_mine), two.step(res_mine)]
    res_rows = core_join(res_mine, swap(res_mine, "core"))
    fed_theirs = swap(short(after(fed_other, res_mine)), "x")
    fed_own = summed_rows(fed_own)
    d_up_bias = row_total(hid_own) + row_total(hid_other)

    def exchange(rows):
        rows = rows.reshape(2, part_rows, -1)
        keep = lax.dynamic_index_in_dim(rows, at_x, 0, False)
        send = lax.dynamic_index_in_dim(rows, 1 - at_x, 0, False).astype(BF16)
        return keep, swap(send, "x")

    d_cross_att = short(dot(after(res_rows, *moved), w_cross_out, 1, 0))
    d_cross_out = scatter(short(dot(res_rows, cross_attended, 0, 0)), all_way)
    moved = [two.step(d_cross_att), three.step(d_cross_att)]
    one = exchange(one.step(d_cross_att))
    cq_grad, ckv_grad = attend_back(
        cross_queries,
        cross_kvs,
        cross_columns,
        width,
        cross_attended,
        after(d_cross_att, *moved),
        logs_cross,
        row_docs,
        col_docs,
        False,
    )
    d_norm_two = summed(dot(cq_grad, w_cross_query, 1, 1))
    d_memory_part = dot(ckv_grad, w_cross_kv, 1, 1)
    moved = [four.step(cq_grad), three.step(cq_grad), d_cross_out.step(cq_grad)]
    d_cross_kv = scatter(short(dot(after(mem_rows, *moved), ckv_grad, 0, 0)), all_way)
    d_cross_query = scatter(short(dot(norm_two, cq_grad, 0, 0)), all_way)
    two = exchange(two.step(cq_grad))
    d_memory = short(summed_rows(d_memory_part))
    back_rows, d_gain_one, d_bias_two = back_two(d_norm_two)
    d_self_res = res_rows.astype(F32) + back_rows
    d_bias_one = row_total(d_self_res)
    self_rows = short(d_self_res)

    d_attended = short(dot(self_rows, w_out, 1, 0))
    d_self_out = scatter(short(dot(self_rows, attended, 0, 0)), all_way)
    moved = [four.step(d_attended), d_cross_out.step(d_attended), d_cross_kv.step(d_attended)]
    three = exchange(three.step(d_attended))
    (qkv_grad,) = attend_back(
        qkv,
        qkv,
        self_columns,
        width,
        attended,
        after(d_attended, *moved),
        logs_self,
        row_docs,
        row_docs,
        True,
    )
    moved = [
        d_cross_query.step(qkv_grad),
        d_self_out.step(qkv_grad),
        d_cross_kv.step(qkv_grad),
        d_cross_out.step(qkv_grad),
    ]
    four = exchange(four.step(qkv_grad))
    cut = 3 * width // 2
    grad_first = short(dot(after(norm_one, *moved[:2]), qkv_grad[:, :cut], 0, 0))
    d_self_one = scatter(grad_first, all_way)
    grad_first = short(dot(after(norm_one, grad_first), qkv_grad[:, cut:], 0, 0))
    d_self_two = scatter(grad_first, ("y", "x", "zl", "zh"))
    d_norm_one = summed_rows(dot(after(qkv_grad, grad_first), w_first, 1, 1))
    layer_out = short(after_cross_mine + fed_own + after(fed_theirs, grad_first).astype(F32) + biases[5])
    moved = [
        d_self_one.step(d_norm_one),
        d_self_two.step(d_norm_one),
        d_cross_query.step(d_norm_one),
        d_self_out.step(d_norm_one),
    ]
    _, back_one = jax.vjp(normalize, own_rows(rows_in), gains[0], biases[0])
    back_rows, d_gain_zero, d_bias_zero = back_one(after(d_norm_one, *moved))
    d_tokens = short(own_rows(d_self_res) + back_rows)

    qkv_total = row_total(qkv_grad)
    head_rows = jnp.stack(
        [
            qkv_total[:width],
            qkv_total[2 * width :],
            row_total(cq_grad),
            row_total(ckv_grad)[width:],
        ]
    )
    head_place = jnp.zeros((4, 2, width), F32)
    head_place = lax.dynamic_update_slice(head_place, head_rows[:, None], (0, at_core, 0))
    bias_place = jnp.zeros((2, 2, hidden_part), F32)
    bias_place = lax.dynamic_update_slice(bias_place, d_up_bias[None, None], (at_core, at_x, 0))
    small = jnp.concatenate(
        [
            jnp.stack(
                [
                    d_gain_zero,
                    d_gain_one * 0.5,
                    d_gain_two,
                    d_bias_zero,
                    d_bias_one * 0.5,
                    d_bias_two * 0.5,
                    d_bias_three,
                    d_bias_four,
                    d_bias_five,
                ]
            ),
            head_place.reshape(-1, features),
            bias_place.reshape(-1, features),
        ]
    )
    for axis in ("core", "x", "y", "zl"):
        small = small + swap(small, axis)
    small = line_total(small)
    head_place = small[9 : 9 + head_place.size // features].reshape(head_place.shape)
    bias_place = small[9 + head_place.size // features :].reshape(2, 2 * hidden_part)
    d_head_biases = lax.dynamic_index_in_dim(head_place, at_core, 1, False)
    d_up_bias = lax.dynamic_index_in_dim(bias_place, at_core, 0, False)

    d_self_one.step(d_tokens)
    d_self_two.step(d_tokens)
    d_cross_kv.step(d_tokens)
    d_cross_out = d_cross_out.step(d_tokens)
    d_cross_query.step(d_tokens)
    d_self_out.step(d_tokens)
    d_self_one.step()
    d_self_two.step()
    d_cross_kv = d_cross_kv.step()
    d_cross_query = d_cross_query.step()
    d_self_out = d_self_out.step()
    d_self_proj = jnp.concatenate([d_self_one.step(), d_self_two.step()], 1)

    def joined(left, right):
        return join_pair(
            jnp.concatenate([left[0], right[0]], 1),
            jnp.concatenate([left[1], right[1]], 1).astype(F32),
            at_x,
            1,
        )

    return (
        layer_out[None],
        d_tokens[None],
        d_memory[None],
        small[:3],
        small[3:9],
        d_head_biases,
        jnp.stack([d_self_proj[:, number * width : (number + 1) * width] for number in range(3)]),
        d_self_out.T,
        d_cross_query,
        jnp.stack([d_cross_kv[:, :width], d_cross_kv[:, width:]]),
        d_cross_out.T,
        joined(three, four),
        d_up_bias,
        joined(one, two).T,
    )


def solution(mesh):
    members, cores = mesh.devices.shape
    parts = Mesh(mesh.devices.reshape(members // 8, 2, 2, 2, cores), AXES + ("core",))
    dp = AXES
    in_specs = (
        P(dp, "core", None),
        P(dp, "core", None),
        P(dp, None),
        P(dp, None),
        P(),
        P(),
        P(None, "core"),
        P(None, dp, "core"),
        P("core", dp),
        P(dp, "core"),
        P(None, dp, "core"),
        P("core", dp),
        P(dp, "core"),
        P("core"),
        P("core", dp),
        P(dp, "core", None),
    )
    out_specs = (
        P(dp, "core", None),
        P(dp, "core", None),
        P(dp, "core", None),
        P(),
        P(),
        P(None, "core"),
        P(None, dp, "core"),
        P("core", dp),
        P(dp, "core"),
        P(None, dp, "core"),
        P("core", dp),
        P(dp, "core"),
        P("core"),
        P("core", dp),
    )
    return jax.shard_map(
        per_device,
        mesh=parts,
        in_specs=in_specs,
        out_specs=out_specs,
        check_vma=False,
    )
```
